256 devices in a mesh: wide: 64 (over x_lo, y, z), head: 4 (over x_hi, core).
Axes of the slice: x: 4 (x_hi: 2, x_lo: 2; x = x_hi * 2 + x_lo), y: 4, z: 8, core: 2. Of those that a mesh axis runs over, the one named last changes fastest.
Arguments:
- queries: bfloat16 [24576, 4096], P('wide', 'head'), may hold values from -200 to 200
- keys: bfloat16 [4096, 4096], P('wide', 'head'), may hold values from -16 to 16
- values: bfloat16 [4096, 4096], P('wide', 'head'), may hold values from -24 to 24
- frame_mask: int32 [24576, 64], P('wide'), may hold values from 0 to 1, as said below
- frame_slot: int32 [64], replicated, may hold values from 0 to 63, each once
- out_weight: bfloat16 [4096, 4096], P('head', 'wide'), may hold values from -0.09375 to 0.09375
- residual: bfloat16 [24576, 4096], P('wide', 'head'), may hold values from -3 to 3
- gate: float32 [4096], P('head'), may hold values from -1.5 to 1.5
Outputs:
- updated: bfloat16 [24576, 4096], P('wide', 'head')
The draws below stay inside these ranges and needn't reach their ends.
Inputs may be any that keep to these rules, and one draw needn't show every extreme that they name: `frame_mask`: row r sees exactly the frames whose ids lie below a bound of its own, from 0 to 64.
All inputs are finite; a program needn't handle non-finite values.
Results may differ from the reference program's by a relative error of at most 0.0065.
Values may be sent and summed in bfloat16 or wider, within the bound.
A program may use at most 128 MiB of HBM per device.

```python
import math
import jax
import jax.numpy as jnp
from jax import lax

HSIZE = 128
HEADS = 32
DW = 4096
TOKF = 64
TEXT = 24576
FRAMES = 64
VIS = 4096
HD = 4096


def shared_keys(key):
    return jnp.clip(2.0 * jax.random.normal(key, (VIS, HD), jnp.float32), -16.0, 16.0)


def draw_keys(key, part):
    common = shared_keys(key)
    return common.astype(jnp.bfloat16)


def draw_queries(key, part):
    key = jax.random.fold_in(key, 12)
    key_drawn = jax.random.fold_in(key, 0)
    drawn = jnp.clip(jax.random.normal(key_drawn, (TEXT, HD), jnp.float32), -6.0, 6.0)
    return drawn.astype(jnp.bfloat16)


def draw_frame_mask(key, part):
    key = jax.random.fold_in(key, 13)
    bound_of_row = jax.random.randint(key, (TEXT, 1), 0, FRAMES + 1)
    return (jnp.arange(FRAMES, dtype=jnp.int32)[None, :] < bound_of_row).astype(jnp.int32)


def level_of(stream_key, dims, shards, least, high):
    factor_of, own = 1.0, jax.random.fold_in(stream_key, 6)
    for dim, blocks in shards:
        steps = jnp.exp(jax.random.uniform(jax.random.fold_in(own, dim), (blocks,), jnp.float32, least / len(shards), high / len(shards)))
        factor_of = factor_of * jnp.repeat(steps, dims[dim] // blocks).reshape([-1 if axis == dim else 1 for axis in range(len(dims))])
    return factor_of


def normal_values(rng, extent, deviation, bound, pieces=(), kind=jnp.bfloat16):
    factor_of = level_of(rng, extent, pieces, -0.22, 0.18) if pieces else 1.0
    entries = jax.random.normal(rng, extent, jnp.float32) * deviation * factor_of
    return jnp.minimum(jnp.maximum(entries, -bound), bound).astype(kind)


def setup_inputs(seed: int = 0) -> dict:
    seeds = jax.random.split(jax.random.key(seed), 9)
    return {
        "queries": draw_queries(jax.random.fold_in(seeds[8], 71), 0),
        "keys": draw_keys(jax.random.fold_in(seeds[8], 71), 0),
        "values": normal_values(seeds[2], (VIS, HD), 4.0, 24.0, ((0, 64), (1, 4))),
        "frame_mask": draw_frame_mask(jax.random.fold_in(seeds[8], 71), 0),
        "frame_slot": jax.random.permutation(seeds[4], FRAMES).astype(jnp.int32),
        "out_weight": normal_values(seeds[5], (HD, DW), HD ** -0.5, 0.09375, ((0, 4), (1, 64))),
        "residual": normal_values(seeds[6], (TEXT, DW), 0.5, 3.0, ((0, 64), (1, 4))),
        "gate": jnp.clip(jax.random.uniform(seeds[7], (DW,), jnp.float32, -1.5, 1.5) * level_of(seeds[7], (DW,), ((0, 4),), -0.4, 0.0), -1.5, 1.5),
    }


def one_head(query_head, key_head, value_head, visible):
    scores = jnp.dot(query_head, key_head.T, preferred_element_type=jnp.float32) * (1.0 / math.sqrt(HSIZE))
    row_max = lax.optimization_barrier(jnp.max(jnp.where(visible, scores, -1e+30), axis=1, keepdims=True))
    weights = jnp.exp(jnp.where(visible, scores - row_max, -1e+30))
    total = lax.optimization_barrier(jnp.sum(weights, axis=1))
    mixed = jnp.dot(weights.astype(jnp.bfloat16), value_head, preferred_element_type=jnp.float32)
    return (mixed, total)

def reference(queries, keys, values, frame_mask, frame_slot, out_weight, residual, gate):
    slot_frames = frame_mask[:, frame_slot]
    visible = jnp.repeat(slot_frames, TOKF, axis=1) > 0
    seen_count = lax.optimization_barrier(jnp.sum(frame_mask, axis=1))
    empty_row = (seen_count == 0).astype(jnp.float32)

    def head_step(running, head_index):
        offset = (head_index * HSIZE).astype(jnp.int32)
        query_head = lax.dynamic_slice_in_dim(queries, offset, HSIZE, 1)
        key_head = lax.dynamic_slice_in_dim(keys, offset, HSIZE, 1)
        value_head = lax.dynamic_slice_in_dim(values, offset, HSIZE, 1)
        mixed, total = one_head(query_head, key_head, value_head, visible)
        attended = (mixed / (total + empty_row)[:, None]).astype(jnp.bfloat16)
        weight_rows = lax.dynamic_slice_in_dim(out_weight, offset, HSIZE, 0)
        return (running + jnp.dot(attended, weight_rows, preferred_element_type=jnp.float32), None)
    initial = jnp.zeros((queries.shape[0], out_weight.shape[1]), jnp.float32)
    projected, _ = lax.scan(head_step, initial, jnp.arange(HEADS, dtype=jnp.int32))
    updated = residual.astype(jnp.float32) + jnp.tanh(gate)[None, :] * projected
    return updated.astype(jnp.bfloat16)
```

```python
import functools
import math

import jax
import jax.numpy as jnp
from jax import lax
from jax.experimental import pallas as pl
from jax.experimental.pallas import tpu as pltpu
from jax.sharding import Mesh, PartitionSpec as P

HSIZE = 128
TOKF = 64
MESH = pl.DeviceIdType.MESH
AXES = ("xl", "y", "z", "xh", "core")
NY, NZ = 4, 8
NG = 8
CHUNK = NG * TOKF
HIDDEN = -1e30
FLOOR = -1e29
LOG2E_SCALE = 1.0 / (math.log(2.0) * math.sqrt(HSIZE))
ROWS = 384
FEATS = 4096
COLS = 1024
A_FEATS = 2048
STREAM = 4


def _kernel(
    q_ref, k_ref, v_ref, bnd_ref, oh_ref, w_ref, res_ref, gate_ref, out_ref,
    k2, vbuf, vt, qbuf, bbuf, qt, m_sc, l_sc, acc, satt, att, wt, wsib,
    loc, ka_s, ka_r, va_s, va_r, q_s, q_r, b_s, b_r, kv_s, kv_r,
    w0_s, w0_r, wx_s, wx_r, wya_s, wya_r, wza_s, wza_r, wzb_s, wzb_r, wyb_s, wyb_r,
    at_s, at_r, sb_s, sb_r,
):
    xl, y, z = lax.axis_index("xl"), lax.axis_index("y"), lax.axis_index("z")
    xh, core = lax.axis_index("xh"), lax.axis_index("core")
    g = xl * NY + y
    head = xh * 2 + core
    ylo = lax.rem(y, 2)
    home = core == y // 2
    away = core != y // 2

    def group(off):
        p = lax.rem(g + off + NG, NG)
        return p, (p // NY, lax.rem(p, NY), z, xh, core)

    def across(off, other):
        p = lax.rem(g + off + NG, NG)
        return (p // NY, lax.rem(p, NY), z, 1 - xh if other else xh, core)

    def zpeer(d):
        return (xl, y, lax.rem(z + d + NZ, NZ), xh, core)

    def ypeer(d):
        return (xl, lax.rem(y + d + NY, NY), z, xh, core)

    sibling = (xl, y, z, xh, 1 - core)

    def remote(src, dst, s, r, dev):
        return pltpu.make_async_remote_copy(
            src_ref=src, dst_ref=dst, send_sem=s, recv_sem=r, device_id=dev, device_id_type=MESH
        )

    bar = pltpu.get_barrier_semaphore()
    for off in range(1, NG):
        pl.semaphore_signal(bar, 1, device_id=group(off)[1], device_id_type=MESH)
    for off in range(NG):
        pl.semaphore_signal(bar, 1, device_id=across(off, True), device_id_type=MESH)
    for d in (1, -1):
        pl.semaphore_signal(bar, 1, device_id=zpeer(d), device_id_type=MESH)
    pl.semaphore_signal(bar, 1, device_id=sibling, device_id_type=MESH)
    pl.semaphore_wait(bar, 18)

    def tok_rows(i):
        return pl.ds(pl.multiple_of(i * TOKF, TOKF), TOKF)

    def head_cols(i):
        return pl.ds(pl.multiple_of(i * HSIZE, HSIZE), HSIZE)

    def k_copy(s, p, dev, src_g):
        return remote(k_ref.at[:, head_cols(p)], k2.at[z, tok_rows(src_g), 0:HSIZE], ka_s.at[s], ka_r.at[s], dev)

    def v_copy(s, p, dev, src_g):
        return remote(v_ref.at[:, head_cols(p)], vbuf.at[z, tok_rows(src_g), :], va_s.at[s], va_r.at[s], dev)

    def q_copy(s, p, dev):
        return remote(q_ref.at[:, head_cols(p)], qbuf.at[7 - s], q_s.at[s], q_r.at[s], dev)

    def b_copy(s, dev):
        return remote(bnd_ref, bbuf.at[7 - s], b_s.at[s], b_r.at[s], dev)

    w0 = remote(w_ref, wsib, w0_s, w0_r, sibling)

    @pl.when(away)
    def _():
        w0.start()

    for s in range(1, NG):
        p, dev = group(s)
        k_copy(s, p, dev, g).start()
        v_copy(s, p, dev, g).start()
    k_own = pltpu.make_async_copy(k_ref.at[:, head_cols(g)], k2.at[z, tok_rows(g), 0:HSIZE], loc.at[0])
    v_own = pltpu.make_async_copy(v_ref.at[:, head_cols(g)], vbuf.at[z, tok_rows(g), :], loc.at[1])
    q_own = pltpu.make_async_copy(q_ref.at[:, head_cols(g)], qbuf.at[7], loc.at[2])
    k_own.start()
    v_own.start()
    q_own.start()
    for s in range(1, NG):
        p, dev = group(s)
        q_copy(s, p, dev).start()
        b_copy(s, dev).start()

    def fill(i, _):
        zi, bi = i // NG, lax.rem(i, NG)
        k2[zi, tok_rows(bi), HSIZE : 2 * HSIZE] = jnp.broadcast_to(
            oh_ref[pl.ds(i, 1), :], (TOKF, HSIZE)
        ).astype(jnp.bfloat16)
        return 0

    lax.fori_loop(0, NZ * NG, fill, 0)
    m_sc[...] = jnp.full(m_sc.shape, FLOOR, jnp.float32)
    l_sc[...] = jnp.zeros(l_sc.shape, jnp.float32)
    acc[...] = jnp.zeros(acc.shape, jnp.float32)
    qt[HSIZE : 2 * HSIZE, :] = jnp.zeros((HSIZE, NG * ROWS), jnp.bfloat16)
    bbuf[7] = bnd_ref[...]

    def feat_cols(h):
        return pl.ds(pl.multiple_of(h * COLS, COLS), COLS)

    def wx_copy(src, c, t):
        h = xh * 2 + c
        return remote(src, wt.at[ylo, z, :, feat_cols(h)], wx_s.at[c, t], wx_r.at[xh, c], (t, y, z, xl, core))

    def wx_self(src, c):
        h = xh * 2 + c
        return pltpu.make_async_copy(src, wt.at[ylo, z, :, feat_cols(h)], wx_r.at[xh, c])

    def wx_each(own, act):
        for t in range(2):
            is_self = jnp.logical_and(xl == xh, xl == t)
            for which in range(2):
                src = w_ref if which == 0 else wsib
                c = core if which == 0 else 1 - core

                @pl.when(jnp.logical_and(home, is_self))
                def _():
                    if own:
                        act(wx_self(src, c))

                @pl.when(jnp.logical_and(home, jnp.logical_not(is_self)))
                def _():
                    act(wx_copy(src, c, t))

    @pl.when(home)
    def _():
        w0.wait_recv()

    wx_each(True, lambda cp: cp.start())

    def kv_piece(slot, which):
        return k2.at[slot, :, 0:HSIZE] if which == 0 else vbuf.at[slot]

    def slot_of(d, r):
        return lax.rem(z - d * r + 2 * NZ, NZ)

    def ring_dirs(r, which):
        if r < 4:
            return (1, -1)
        return (1,) if which == 0 else (-1,)

    def kv_send(d, r, which):
        slot = slot_of(d, r - 1)
        ref = kv_piece(slot, which)
        i = 0 if d == 1 else 1
        return remote(ref, ref, kv_s.at[i, r, which], kv_r.at[i, r, which], zpeer(d))

    def kv_recv(d, r, which):
        slot = slot_of(d, r)
        ref = kv_piece(slot, which)
        i = 0 if d == 1 else 1
        return remote(ref, ref, kv_s.at[i, r, which], kv_r.at[i, r, which], zpeer(d))

    for which in range(2):
        for s in range(1, NG):
            src, _unused = group(-s)
            if which == 0:
                k_copy(s, 0, sibling, src).wait_recv()
            else:
                v_copy(s, 0, sibling, src).wait_recv()
        (k_own if which == 0 else v_own).wait()
        for d in ring_dirs(1, which):
            kv_send(d, 1, which).start()

    def wya_copy(lo, d):
        ref = wt.at[lo, z, :, 0:A_FEATS]
        return remote(ref, ref, wya_s.at[d], wya_r.at[lo], ypeer(d))

    def wza_half(slot, half):
        if half is None:
            return wt.at[:, slot, :, 0:A_FEATS]
        return wt.at[half, slot, :, 0:A_FEATS]

    def wzb_half(slot, half):
        if half is None:
            return wt.at[ylo, slot, :, A_FEATS:FEATS]
        return wt.at[ylo, slot, 32 * half : 32 * half + 32, A_FEATS:FEATS]

    def wz_copy(piece, s, r, d, rnd, sending):
        slot = slot_of(d, rnd - 1) if sending else slot_of(d, rnd)
        i = 0 if d == 1 else 1
        ref = piece(slot, None if rnd < 4 else i)
        return remote(ref, ref, s.at[i, rnd], r.at[i, rnd], zpeer(d))

    def wza(d, rnd, sending):
        return wz_copy(wza_half, wza_s, wza_r, d, rnd, sending)

    def wzb(d, rnd, sending):
        return wz_copy(wzb_half, wzb_s, wzb_r, d, rnd, sending)

    def wyb_copy(lo, slot, n, d):
        ref = wt.at[lo, slot, :, A_FEATS:FEATS]
        return remote(ref, ref, wyb_s.at[n, d], wyb_r.at[lo, n], ypeer(d))

    def nth_slot(n):
        return lax.rem(z + (0, -1, 1, -2, 2, -3, 3, 4)[n] + NZ, NZ)

    @pl.when(home)
    def _():
        for xs in range(2):
            for c in range(2):
                ref = wt.at[ylo, z, :, feat_cols(xs * 2 + c)]
                pltpu.make_async_copy(ref, ref, wx_r.at[xs, c]).wait()
        for d in (1, 3, 2):
            wya_copy(ylo, d).start()
        for d in (1, -1):
            wzb(d, 1, True).start()
        for d in (1, 3, 2):
            wyb_copy(ylo, nth_slot(0), 0, d).start()

    def queries_in(p):
        cols = slice(p * ROWS, (p + 1) * ROWS)
        qt[0:HSIZE, cols] = qbuf[p].T
        frame = lax.broadcasted_iota(jnp.int32, (TOKF, ROWS), 0).astype(jnp.float32)
        qt[HSIZE : HSIZE + TOKF, cols] = jnp.where(frame < bbuf[p, 0:1, :], 0.0, HIDDEN).astype(
            jnp.bfloat16
        )

    def vt_cols(slot):
        return pl.ds(pl.multiple_of(slot * CHUNK, CHUNK), CHUNK)

    for s in range(7, 0, -1):
        q_copy(s, 0, sibling).wait_recv()
        b_copy(s, sibling).wait_recv()
        queries_in(7 - s)
    q_own.wait()
    queries_in(7)

    wide = slice(0, STREAM * ROWS)

    def stream(slot):
        vt[:, vt_cols(slot)] = vbuf[slot].T
        s = jnp.dot(k2[slot], qt[:, wide], preferred_element_type=jnp.float32)
        m_old = m_sc[0:1, :]
        m_new = jnp.maximum(m_old, jnp.max(s, axis=0, keepdims=True))
        p = jnp.exp2((s - m_new) * LOG2E_SCALE)
        shrink = jnp.exp2((m_old - m_new) * LOG2E_SCALE)
        m_sc[0:1, :] = m_new
        l_sc[0:1, :] = l_sc[0:1, :] * shrink + jnp.sum(p, axis=0, keepdims=True)
        acc[...] = acc[...] * shrink + jnp.dot(
            vt[:, vt_cols(slot)], p.astype(jnp.bfloat16), preferred_element_type=jnp.float32
        )

    def attend(n):
        stream(nth_slot(n))

    attend(0)
    for rnd in range(1, 5):
        for which in range(2):
            for d in ring_dirs(rnd, which):
                kv_recv(d, rnd, which).wait_recv()
            if rnd < 4:
                for d in ring_dirs(rnd + 1, which):
                    kv_send(d, rnd + 1, which).start()

        @pl.when(home)
        def _():
            for i, d in enumerate((1, -1)):
                wzb(d, rnd, False).wait_recv()
                if rnd < 4:
                    wzb(d, rnd + 1, True).start()
                    n = 2 * rnd - 1 + i
                    for e in (1, 3, 2):
                        wyb_copy(ylo, nth_slot(n), n, e).start()
            if rnd == 4:
                for e in (1, 3, 2):
                    wyb_copy(ylo, nth_slot(7), 7, e).start()

        if rnd == 2:
            for lo in range(2):

                @pl.when(y != core * 2 + lo)
                def _():
                    wya_copy(lo, 1).wait_recv()

            for d in (1, -1):
                wza(d, 1, True).start()
        attend(2 * rnd - 1)
        if rnd < 4:
            attend(2 * rnd)

    def att_rows(h, p):
        return pl.ds(pl.multiple_of((h * NG + p) * HSIZE, HSIZE), HSIZE)

    def att_copy(off, other, h, src_g):
        i = 1 if other else 0
        return remote(
            satt.at[(off + 7) % 8], att.at[att_rows(h, src_g), :], at_s.at[i, off], at_r.at[i, off], across(off, other)
        )

    att_own = pltpu.make_async_copy(satt.at[7], att.at[att_rows(head, g), :], loc.at[3])

    def give(p):
        off = (p + 1) % 8
        att_copy(off, True, head, g).start()
        if off == 0:
            att_own.start()
        else:
            att_copy(off, False, head, g).start()

    def normed(p, mixed, total):
        empty = (bbuf[p, 0:1, :] == 0.0).astype(jnp.float32)
        satt[p] = (mixed / (total + empty)).astype(jnp.bfloat16)

    for p in range(STREAM):
        cols = slice(p * ROWS, (p + 1) * ROWS)
        normed(p, acc[:, cols], l_sc[0:1, cols])
        give(p)

    def wza_step(rnd):
        for d in (1, -1):
            wza(d, rnd, False).wait_recv()
            if rnd < 4:
                wza(d, rnd + 1, True).start()

    for p in range(STREAM, NG):
        s = jnp.dot(
            k2[...].reshape(NZ * CHUNK, 2 * HSIZE),
            qt[:, p * ROWS : (p + 1) * ROWS],
            preferred_element_type=jnp.float32,
        )
        m_all = jnp.maximum(jnp.max(s, axis=0, keepdims=True), FLOOR)
        w = jnp.exp2((s - m_all) * LOG2E_SCALE)
        total = jnp.sum(w, axis=0, keepdims=True)
        mixed = jnp.dot(vt[...], w.astype(jnp.bfloat16), preferred_element_type=jnp.float32)
        normed(p, mixed, total)
        give(p)
        if p == STREAM + 1:
            wza_step(1)
        if p == STREAM + 3:
            wza_step(2)

    def sib_copy(off, other, mine):
        i = 1 if other else 0
        xs = 1 - xh if other else xh
        c = core if mine else 1 - core
        ref = att.at[att_rows(xs * 2 + c, lax.rem(g - off + NG, NG)), :]
        return remote(ref, ref, sb_s.at[i, off], sb_r.at[i, off], sibling)

    for off in (1, 2, 3, 4, 5, 6, 7, 0):
        for other in (False, True):
            if off == 0 and not other:
                att_own.wait()
            else:
                xs = 1 - xh if other else xh
                att_copy(off, other, xs * 2 + core, lax.rem(g - off + NG, NG)).wait_recv()
            sib_copy(off, other, True).start()
    wza_step(3)
    for off in range(NG):
        for other in (False, True):
            sib_copy(off, other, False).wait_recv()
    wza_step(4)
    for lo in range(2):

        @pl.when(y != core * 2 + lo)
        def _():
            for n in range(8):
                wyb_copy(lo, nth_slot(n), n, 1).wait_recv()

    def project(i, _):
        lo, half = i // 2, lax.rem(i, 2)
        w = wt[lo, pl.ds(half * 4, 4)].reshape(256, FEATS)
        part = jnp.dot(w, att[...], preferred_element_type=jnp.float32)
        cols = pl.ds(pl.multiple_of(i * 256, 256), 256)
        out_ref[:, cols] = (
            res_ref[:, cols].astype(jnp.float32) + jnp.tanh(gate_ref[:, cols]) * part.T
        ).astype(out_ref.dtype)
        return 0

    lax.fori_loop(0, 4, project, 0)

    @pl.when(away)
    def _():
        w0.wait_send()

    for t in range(2):
        for which in range(2):
            src = w_ref if which == 0 else wsib
            c = core if which == 0 else 1 - core

            @pl.when(jnp.logical_and(home, jnp.logical_not(jnp.logical_and(xl == xh, xl == t))))
            def _():
                wx_copy(src, c, t).wait_send()

    for s in range(1, NG):
        p, dev = group(s)
        k_copy(s, p, dev, g).wait_send()
        v_copy(s, p, dev, g).wait_send()
        q_copy(s, p, dev).wait_send()
        b_copy(s, dev).wait_send()
    for rnd in range(1, 5):
        for which in range(2):
            for d in ring_dirs(rnd, which):
                kv_send(d, rnd, which).wait_send()
        for d in (1, -1):
            wza(d, rnd, True).wait_send()

    @pl.when(home)
    def _():
        for d in (1, 3, 2):
            wya_copy(ylo, d).wait_send()
        for rnd in range(1, 5):
            for d in (1, -1):
                wzb(d, rnd, True).wait_send()
        for n in range(8):
            for d in (1, 3, 2):
                wyb_copy(ylo, nth_slot(n), n, d).wait_send()

    for off in range(NG):
        for other in (False, True):
            if other or off:
                att_copy(off, other, head, g).wait_send()
            sib_copy(off, other, True).wait_send()


def _on_device(queries, keys, values, frame_mask, frame_slot, out_weight, residual, gate):
    seen = jnp.sum(frame_mask, axis=1).astype(jnp.float32)
    bounds = jnp.broadcast_to(seen[None, :], (8, ROWS))
    order = frame_slot.reshape(NG, NZ).T.reshape(NG * NZ)
    onehot = (order[:, None] == jnp.arange(HSIZE, dtype=jnp.int32)[None, :]).astype(jnp.float32)
    dma = pltpu.SemaphoreType.DMA
    vmem = pl.BlockSpec(memory_space=pltpu.VMEM)
    hbm = pl.BlockSpec(memory_space=pl.ANY)
    bf16, f32 = jnp.bfloat16, jnp.float32
    return pl.pallas_call(
        _kernel,
        out_shape=jax.ShapeDtypeStruct((ROWS, COLS), bf16),
        in_specs=[hbm, hbm, hbm, vmem, vmem, vmem, vmem, vmem],
        out_specs=vmem,
        scratch_shapes=[
            pltpu.VMEM((NZ, CHUNK, 2 * HSIZE), bf16),
            pltpu.VMEM((NZ, CHUNK, HSIZE), bf16),
            pltpu.VMEM((HSIZE, NZ * CHUNK), bf16),
            pltpu.VMEM((NG, ROWS, HSIZE), bf16),
            pltpu.VMEM((NG, 8, ROWS), f32),
            pltpu.VMEM((2 * HSIZE, NG * ROWS), bf16),
            pltpu.VMEM((8, STREAM * ROWS), f32),
            pltpu.VMEM((8, STREAM * ROWS), f32),
            pltpu.VMEM((HSIZE, STREAM * ROWS), f32),
            pltpu.VMEM((NG, HSIZE, ROWS), bf16),
            pltpu.VMEM((FEATS, ROWS), bf16),
            pltpu.VMEM((2, NZ, TOKF, FEATS), bf16),
            pltpu.VMEM((TOKF, COLS), bf16),
            dma((4,)),
            dma((8,)), dma((8,)), dma((8,)), dma((8,)),
            dma((8,)), dma((8,)), dma((8,)), dma((8,)),
            dma((2, 5, 2)), dma((2, 5, 2)),
            dma, dma,
            dma((2, 2)), dma((2, 2)),
            dma((4,)), dma((2,)),
            dma((2, 5)), dma((2, 5)),
            dma((2, 5)), dma((2, 5)),
            dma((8, 4)), dma((2, 8)),
            dma((2, 8)), dma((2, 8)),
            dma((2, 8)), dma((2, 8)),
        ],
        compiler_params=pltpu.CompilerParams(
            collective_id=0, has_side_effects=True, vmem_limit_bytes=58 * 2**20
        ),
    )(queries, keys, values, bounds, onehot, out_weight.T, residual, gate.reshape(1, COLS))


def solution(mesh):
    fine = Mesh(mesh.devices.reshape(2, NY, NZ, 2, 2), AXES)
    wide, head = ("xl", "y", "z"), ("xh", "core")
    return jax.shard_map(
        _on_device,
        mesh=fine,
        in_specs=(
            P(wide, head),
            P(wide, head),
            P(wide, head),
            P(wide, None),
            P(),
            P(head, wide),
            P(wide, head),
            P(head),
        ),
        out_specs=P(wide, head),
        check_vma=False,
    )
```

```python
import functools
import math

import jax
import jax.numpy as jnp
from jax import lax
from jax.experimental import pallas as pl
from jax.experimental.pallas import tpu as pltpu
from jax.sharding import Mesh, PartitionSpec as P

HSIZE = 128
TOKF = 64
MESH = pl.DeviceIdType.MESH
AXES = ("xl", "y", "z", "xh", "core")
NY, NZ = 4, 8
NG = 8
CHUNK = NG * TOKF
HIDDEN = -1e30
FLOOR = -1e29
LOG2E_SCALE = 1.0 / (math.log(2.0) * math.sqrt(HSIZE))
ROWS = 384
FEATS = 4096
COLS = 1024
OWN = 512
STREAM = 4
ORDER = (0, 2, 1, 3)
PLACE = {(dy, o): 2 * i + o for i, dy in enumerate(ORDER) for o in range(2)}
PLANE = tuple((dy, o) for dy in ORDER for o in range(2) if (dy, o) != (0, 0))


def _kernel(
    q_ref, k_ref, v_ref, mask_ref, slot_ref, w_ref, res_ref, gate_ref, out_ref,
    k2, vbuf, vt, qbuf, bnd, bbuf, qt, m_sc, l_sc, acc, satt, att, wt, wown, res, res2, upd,
    loc, ka_s, ka_r, va_s, va_r, q_s, q_r, b_s, b_r, kv_s, kv_r,
    wx_s, wx_r, wr_s, wr_r, wy_s, wy_r, rl_s,
    t1_s, t1_r, t2_s, t2_r, t3_s, t3_r, sb_s, sb_r, rs_s, rs_r, up_s, up_r,
):
    xl, y, z = lax.axis_index("xl"), lax.axis_index("y"), lax.axis_index("z")
    xh, core = lax.axis_index("xh"), lax.axis_index("core")
    g = xl * NY + y
    head = xh * 2 + core
    ylo = lax.rem(y, 2)
    home = jnp.logical_and(core == y // 2, xl == ylo)

    def ypos(d):
        return lax.rem(y + d + NY, NY)

    def zpos(d):
        return lax.rem(z + d + NZ, NZ)

    def dev(other_xl=0, dy=0, dz=0, other_xh=0, other_core=0):
        return (
            1 - xl if other_xl else xl,
            ypos(dy),
            zpos(dz),
            1 - xh if other_xh else xh,
            1 - core if other_core else core,
        )

    def remote(src, dst, s, r, to):
        return pltpu.make_async_remote_copy(
            src_ref=src, dst_ref=dst, send_sem=s, recv_sem=r, device_id=to, device_id_type=MESH
        )

    sibling = dev(other_core=1)

    bar = pltpu.get_barrier_semaphore()
    peers = [dev(other_xl=o, dy=dy) for dy, o in PLANE]
    peers += [dev(dz=1), dev(dz=-1), sibling]
    peers += [dev(other_xl=o, other_xh=1) for o in (0, 1)]
    peers += [dev(other_xl=o, other_xh=h, other_core=1) for o, h in ((0, 1), (1, 0), (1, 1))]
    for to in peers:
        pl.semaphore_signal(bar, 1, device_id=to, device_id_type=MESH)

    def own_copy(src, dst, i):
        return pltpu.make_async_copy(src, dst, loc.at[i])

    wown[...] = w_ref[...].T
    ones = jnp.ones((8, mask_ref.shape[1]), jnp.bfloat16)
    bnd[...] = lax.dot_general(
        ones, mask_ref[...].astype(jnp.bfloat16), (((1,), (1,)), ((), ())), preferred_element_type=jnp.float32
    )
    bbuf[PLACE[(0, 0)]] = bnd[...]
    pl.semaphore_wait(bar, len(peers))

    def feat_cols(h):
        return pl.ds(pl.multiple_of(h * COLS, COLS), COLS)

    wx_copy = remote(wown, wt.at[z, :, feat_cols(head)], wx_s, wx_r.at[head], (ylo, y, z, xl, y // 2))
    wx_own = pltpu.make_async_copy(wown, wt.at[z, :, feat_cols(head)], wx_r.at[head])
    wx_is_self = jnp.logical_and(home, xl == xh)

    def tok_rows(i):
        return pl.ds(pl.multiple_of(i * TOKF, TOKF), TOKF)

    def head_cols(i):
        return pl.ds(pl.multiple_of(i * HSIZE, HSIZE), HSIZE)

    def group(dy, o):
        return (1 - xl if o else xl) * NY + ypos(dy)

    def k_copy(i, dy, o, src_g):
        return remote(
            k_ref.at[:, head_cols(group(dy, o))], k2.at[z, tok_rows(src_g), 0:HSIZE],
            ka_s.at[i], ka_r.at[i], dev(other_xl=o, dy=dy),
        )

    def v_copy(i, dy, o, src_g):
        return remote(
            v_ref.at[:, head_cols(group(dy, o))], vbuf.at[z, tok_rows(src_g), :],
            va_s.at[i], va_r.at[i], dev(other_xl=o, dy=dy),
        )

    def q_copy(i, dy, o):
        return remote(
            q_ref.at[:, head_cols(group(dy, o))], qbuf.at[PLACE[(-dy % NY, o)]],
            q_s.at[i], q_r.at[i], dev(other_xl=o, dy=dy),
        )

    def b_copy(i, dy, o):
        return remote(bnd, bbuf.at[PLACE[(-dy % NY, o)]], b_s.at[i], b_r.at[i], dev(other_xl=o, dy=dy))

    def window(i):
        return pl.ds(pl.multiple_of(i * OWN, OWN), OWN)

    k_own = own_copy(k_ref.at[:, head_cols(g)], k2.at[z, tok_rows(g), 0:HSIZE], 0)
    v_own = own_copy(v_ref.at[:, head_cols(g)], vbuf.at[z, tok_rows(g), :], 1)
    q_own = own_copy(q_ref.at[:, head_cols(g)], qbuf.at[PLACE[(0, 0)]], 2)
    res_in = own_copy(res_ref.at[:, window(xl)], res, 3)
    partner = dev(other_xl=1)
    res_out = remote(res_ref.at[:, window(1 - xl)], res2, rs_s, rs_r, partner)
    for i, (dy, o) in enumerate(PLANE):
        k_copy(i, dy, o, g).start()
    for i, (dy, o) in enumerate(PLANE):
        v_copy(i, dy, o, g).start()
    k_own.start()
    v_own.start()

    @pl.when(wx_is_self)
    def _():
        wx_own.start()

    @pl.when(jnp.logical_not(wx_is_self))
    def _():
        wx_copy.start()

    for i, (dy, o) in enumerate(PLANE):
        q_copy(i, dy, o).start()
        b_copy(i, dy, o).start()
    q_own.start()
    res_in.start()
    res_out.start()

    lane = lax.broadcasted_iota(jnp.int32, (TOKF, HSIZE), 1)

    def fill(i, _):
        zi, bi = i // NG, lax.rem(i, NG)
        k2[zi, tok_rows(bi), HSIZE : 2 * HSIZE] = jnp.where(lane == slot_ref[bi * NZ + zi], 1.0, 0.0).astype(
            jnp.bfloat16
        )
        return 0

    lax.fori_loop(0, NZ * NG, fill, 0)
    m_sc[...] = jnp.full(m_sc.shape, FLOOR, jnp.float32)
    l_sc[...] = jnp.zeros(l_sc.shape, jnp.float32)
    acc[...] = jnp.zeros(acc.shape, jnp.float32)
    qt[HSIZE : 2 * HSIZE, :] = jnp.zeros((HSIZE, NG * ROWS), jnp.bfloat16)

    def ring_dirs(r, which):
        if r < 4:
            return (1, -1)
        return (1,) if which == 0 else (-1,)

    class Ring:
        def __init__(self, piece, s, r):
            self.piece, self.s, self.r = piece, s, r

        def copy(self, d, r, which, steps):
            ref = self.piece(lax.rem(z - d * steps + 2 * NZ, NZ), which)
            i = 0 if d == 1 else 1
            return remote(ref, ref, self.s.at[i, r, which], self.r.at[i, r, which], dev(dz=d))

        def send(self, d, r, which):
            return self.copy(d, r, which, r - 1)

        def begin(self, which):
            for d in ring_dirs(1, which):
                self.send(d, 1, which).start()

        def step(self, r, pieces=(0, 1)):
            for which in pieces:
                for d in ring_dirs(r, which):
                    self.copy(d, r, which, r).wait_recv()
                    if r < 4 and d in ring_dirs(r + 1, which):
                        self.send(d, r + 1, which).start()

        def end(self):
            for r in range(1, 5):
                for which in range(2):
                    for d in ring_dirs(r, which):
                        self.send(d, r, which).wait_send()

    def half(which):
        return slice(32 * which, 32 * which + 32)

    kv_ring = Ring(lambda slot, w: vbuf.at[slot] if w else k2.at[slot, :, 0:HSIZE], kv_s, kv_r)
    w_ring = Ring(lambda slot, w: wt.at[slot, half(w)], wr_s, wr_r)

    def wy_copy(which, d, s):
        ref = wt.at[z, half(which)]
        return remote(ref, ref, s, wy_r.at[which], dev(dy=d))

    def wy_send(which, i):
        return wy_copy(which, (1, -1)[i], wy_s.at[which, i])

    place = lax.rem(y - 2 * core - xl + 2 * NY, NY)

    def relay_copy(which):
        return wy_copy(which, (1, -1)[which], rl_s)

    def relay():
        for which in range(2):

            @pl.when(place == (1, 3)[which])
            def _():
                wy_copy(which, 1, rl_s).wait_recv()
                relay_copy(which).start()

    def relayed():
        for which in range(2):

            @pl.when(jnp.logical_or(place == 2, place == (3, 1)[which]))
            def _():
                wy_copy(which, 1, rl_s).wait_recv()

    for i, (dy, o) in enumerate(PLANE):
        k_copy(i, dy, o, group(-dy, o)).wait_recv()
    k_own.wait()
    kv_ring.begin(0)
    for i, (dy, o) in enumerate(PLANE):
        v_copy(i, dy, o, group(-dy, o)).wait_recv()
    v_own.wait()
    kv_ring.begin(1)

    @pl.when(home)
    def _():
        for h in range(4):
            ref = wt.at[z, :, feat_cols(h)]
            pltpu.make_async_copy(ref, ref, wx_r.at[h]).wait()
        for which in range(2):
            for i in range(2):
                wy_send(which, i).start()

    kv_ring.step(1)
    relay()

    def queries_in(p):
        cols = slice(p * ROWS, (p + 1) * ROWS)
        qt[0:HSIZE, cols] = qbuf[p].T
        frame = lax.broadcasted_iota(jnp.int32, (TOKF, ROWS), 0).astype(jnp.float32)
        qt[HSIZE : HSIZE + TOKF, cols] = jnp.where(frame < bbuf[p, 0:1, :], 0.0, HIDDEN).astype(
            jnp.bfloat16
        )

    for i, (dy, o) in enumerate(PLANE):
        q_copy(i, dy, o).wait_recv()
        b_copy(i, dy, o).wait_recv()
        queries_in(PLACE[(-dy % NY, o)])
    q_own.wait()
    queries_in(PLACE[(0, 0)])

    def vt_cols(slot):
        return pl.ds(pl.multiple_of(slot * CHUNK, CHUNK), CHUNK)

    def attend(n):
        slot = zpos((0, -1, 1, -2, 2, -3, 3, 4)[n])
        vt[:, vt_cols(slot)] = vbuf[slot].T
        s = jnp.dot(k2[slot], qt[:, 0 : STREAM * ROWS], preferred_element_type=jnp.float32)
        m_old = m_sc[0:1, :]
        m_new = jnp.maximum(m_old, jnp.max(s, axis=0, keepdims=True))
        p = jnp.exp2((s - m_new) * LOG2E_SCALE)
        shrink = jnp.exp2((m_old - m_new) * LOG2E_SCALE)
        m_sc[0:1, :] = m_new
        l_sc[0:1, :] = l_sc[0:1, :] * shrink + jnp.sum(p, axis=0, keepdims=True)
        acc[...] = acc[...] * shrink + jnp.dot(
            vt[:, vt_cols(slot)], p.astype(jnp.bfloat16), preferred_element_type=jnp.float32
        )

    def head_slot(other_xl, other_xh, dy, other_core=0, part=None):
        h = (1 - xh if other_xh else xh) * 2 + (1 - core if other_core else core)
        p = h * NG + (1 - xl if other_xl else xl) * NY + ypos(-dy)
        if part is None:
            return att.at[pl.ds(pl.multiple_of(p * HSIZE, HSIZE), HSIZE), :]
        return att.at[pl.ds(pl.multiple_of(p * HSIZE + part * 64, 64), 64), :]

    def t1_copy(dy):
        return remote(satt.at[dy], head_slot(0, 0, 0), t1_s.at[dy], t1_r.at[dy], dev(dy=dy))

    def t1_got(dy):
        return remote(satt.at[dy], head_slot(0, 0, dy), t1_s.at[dy], t1_r.at[dy], sibling)

    def t2_copy(dy, h):
        src = head_slot(0, 0, dy) if dy else satt.at[0]
        return remote(src, head_slot(0, 0, dy), t2_s.at[dy, h], t2_r.at[dy, h], dev(other_xl=1, other_xh=h))

    def t2_got(dy, h):
        ref = head_slot(1, h, dy)
        return remote(ref, ref, t2_s.at[dy, h], t2_r.at[dy, h], sibling)

    def t3_copy(dy, h):
        ref = head_slot(1, h, dy, part=h)
        return remote(ref, ref, t3_s.at[dy, h], t3_r.at[dy, h], dev(other_xl=1, other_xh=1 - h))

    def t3_got(dy, h):
        ref = head_slot(0, 1, dy, part=h)
        return remote(ref, ref, t3_s.at[dy, h], t3_r.at[dy, h], sibling)

    def sb_copy(dy, o, h):
        ref = head_slot(o, h, dy)
        return remote(ref, ref, sb_s.at[dy, o, h], sb_r.at[dy, o, h], sibling)

    def sb_got(dy, o, h):
        ref = head_slot(o, h, dy, 1)
        return remote(ref, ref, sb_s.at[dy, o, h], sb_r.at[dy, o, h], sibling)

    att_own = own_copy(satt.at[0], head_slot(0, 0, 0), 4)

    def give(dy):
        if dy:
            t1_copy(dy).start()
        else:
            for h in range(2):
                t2_copy(0, h).start()
            att_own.start()

    def pass_on(dy):
        if dy:
            t1_got(dy).wait_recv()
            for h in range(2):
                t2_copy(dy, h).start()
        else:
            att_own.wait()
        sb_copy(dy, 0, 0).start()

    def take(dy):
        for h in range(2):
            t2_got(dy, h).wait_recv()
            t3_copy(dy, h).start()
            sb_copy(dy, 1, h).start()

    def take_far(dy):
        for h in range(2):
            t3_got(dy, h).wait_recv()
        sb_copy(dy, 0, 1).start()

    def normed(p, mixed, total):
        dy, o = ORDER[p // 2], p % 2
        empty = (bbuf[p, 0:1, :] == 0.0).astype(jnp.float32)
        cols = pl.ds(pl.multiple_of((1 - xl if o else xl) * ROWS, ROWS), ROWS)
        satt[dy, :, cols] = (mixed / (total + empty)).astype(jnp.bfloat16)

    def attend_block(p):
        s = jnp.dot(
            k2[...].reshape(NZ * CHUNK, 2 * HSIZE),
            qt[:, p * ROWS : (p + 1) * ROWS],
            preferred_element_type=jnp.float32,
        )
        m_all = jnp.maximum(jnp.max(s, axis=0, keepdims=True), FLOOR)
        w = jnp.exp2((s - m_all) * LOG2E_SCALE)
        total = jnp.sum(w, axis=0, keepdims=True)
        mixed = jnp.dot(vt[...], w.astype(jnp.bfloat16), preferred_element_type=jnp.float32)
        normed(p, mixed, total)

    attend(0)
    kv_ring.step(2)
    attend(1)
    attend(2)
    relayed()
    kv_ring.step(3)
    for which in range(2):
        w_ring.begin(which)
    attend(3)
    attend(4)
    kv_ring.step(4)
    attend(5)
    attend(6)
    attend(7)
    for p in range(STREAM):
        cols = slice(p * ROWS, (p + 1) * ROWS)
        normed(p, acc[:, cols], l_sc[0:1, cols])
        if p % 2:
            give(ORDER[p // 2])
    w_ring.step(1, (0,))
    attend_block(4)
    pass_on(ORDER[0])
    w_ring.step(1, (1,))
    attend_block(5)
    give(ORDER[2])
    pass_on(ORDER[1])
    take(ORDER[0])
    w_ring.step(2, (0,))
    attend_block(6)
    pass_on(ORDER[2])
    take(ORDER[1])
    w_ring.step(2, (1,))
    attend_block(7)
    give(ORDER[3])
    take_far(ORDER[0])
    w_ring.step(3, (0,))
    take(ORDER[2])
    pass_on(ORDER[3])
    take_far(ORDER[1])
    w_ring.step(3, (1,))
    take(ORDER[3])
    take_far(ORDER[2])
    take_far(ORDER[3])
    w_ring.step(4)
    for dy in ORDER:
        for o in range(2):
            for h in range(2):
                sb_got(dy, o, h).wait_recv()
    res_in.wait()
    res_out.wait_recv()

    def project(i, side, before, put):
        w = wt[4 * i : 4 * i + 4].reshape(256, FEATS)
        rows = pl.ds(pl.multiple_of(side * ROWS, ROWS), ROWS)
        summed = jnp.dot(w, att[:, rows], preferred_element_type=jnp.float32)
        scale = jnp.tanh(gate_ref[:, pl.ds(pl.multiple_of(xl * OWN + i * 256, 256), 256)])
        put((before.astype(jnp.float32) + scale * summed.T).astype(jnp.bfloat16))

    def up_copy(i):
        cols = pl.ds(pl.multiple_of(xl * OWN + i * 256, 256), 256)
        return remote(upd.at[i], out_ref.at[:, cols], up_s.at[i], up_r.at[i], partner)

    def up_got(i):
        cols = pl.ds(pl.multiple_of((1 - xl) * OWN + i * 256, 256), 256)
        return remote(upd.at[i], out_ref.at[:, cols], up_s.at[i], up_r.at[i], partner)

    for i in range(2):

        def put_far(x):
            upd[i] = x

        project(i, 1 - xl, res2[:, 256 * i : 256 * i + 256], put_far)
        up_copy(i).start()
    for i in range(2):

        def put_own(x):
            out_ref[:, pl.ds(pl.multiple_of(xl * OWN + i * 256, 256), 256)] = x

        project(i, xl, res[:, 256 * i : 256 * i + 256], put_own)
    for i in range(2):
        up_got(i).wait_recv()

    @pl.when(jnp.logical_not(wx_is_self))
    def _():
        wx_copy.wait_send()

    for i, (dy, o) in enumerate(PLANE):
        k_copy(i, dy, o, g).wait_send()
        v_copy(i, dy, o, g).wait_send()
        q_copy(i, dy, o).wait_send()
        b_copy(i, dy, o).wait_send()
    res_out.wait_send()
    kv_ring.end()

    w_ring.end()

    @pl.when(home)
    def _():
        for which in range(2):
            for i in range(2):
                wy_send(which, i).wait_send()

    for which in range(2):

        @pl.when(place == (1, 3)[which])
        def _():
            relay_copy(which).wait_send()

    for dy in ORDER:
        if dy:
            t1_copy(dy).wait_send()
        for h in range(2):
            t2_copy(dy, h).wait_send()
            t3_copy(dy, h).wait_send()
            for o in range(2):
                sb_copy(dy, o, h).wait_send()
    for i in range(2):
        up_copy(i).wait_send()


def _on_device(queries, keys, values, frame_mask, frame_slot, out_weight, residual, gate):
    dma = pltpu.SemaphoreType.DMA
    vmem = pl.BlockSpec(memory_space=pltpu.VMEM)
    hbm = pl.BlockSpec(memory_space=pl.ANY)
    smem = pl.BlockSpec(memory_space=pltpu.SMEM)
    bf16, f32 = jnp.bfloat16, jnp.float32
    return pl.pallas_call(
        _kernel,
        out_shape=jax.ShapeDtypeStruct((ROWS, COLS), bf16),
        in_specs=[hbm, hbm, hbm, vmem, smem, vmem, hbm, vmem],
        out_specs=vmem,
        scratch_shapes=[
            pltpu.VMEM((NZ, CHUNK, 2 * HSIZE), bf16),
            pltpu.VMEM((NZ, CHUNK, HSIZE), bf16),
            pltpu.VMEM((HSIZE, NZ * CHUNK), bf16),
            pltpu.VMEM((NG, ROWS, HSIZE), bf16),
            pltpu.VMEM((8, ROWS), f32),
            pltpu.VMEM((NG, 8, ROWS), f32),
            pltpu.VMEM((2 * HSIZE, NG * ROWS), bf16),
            pltpu.VMEM((8, STREAM * ROWS), f32),
            pltpu.VMEM((8, STREAM * ROWS), f32),
            pltpu.VMEM((HSIZE, STREAM * ROWS), f32),
            pltpu.VMEM((NY, HSIZE, 2 * ROWS), bf16),
            pltpu.VMEM((FEATS, 2 * ROWS), bf16),
            pltpu.VMEM((NZ, TOKF, FEATS), bf16),
            pltpu.VMEM((TOKF, COLS), bf16),
            pltpu.VMEM((ROWS, OWN), bf16),
            pltpu.VMEM((ROWS, OWN), bf16),
            pltpu.VMEM((2, ROWS, 256), bf16),
            dma((5,)),
            dma((7,)), dma((7,)), dma((7,)), dma((7,)),
            dma((7,)), dma((7,)), dma((7,)), dma((7,)),
            dma((2, 5, 2)), dma((2, 5, 2)),
            dma, dma((4,)),
            dma((2, 5, 2)), dma((2, 5, 2)),
            dma((2, 2)), dma((2,)), dma,
            dma((4,)), dma((4,)),
            dma((4, 2)), dma((4, 2)),
            dma((4, 2)), dma((4, 2)),
            dma((4, 2, 2)), dma((4, 2, 2)),
            dma, dma,
            dma((2,)), dma((2,)),
        ],
        compiler_params=pltpu.CompilerParams(
            collective_id=0, has_side_effects=True, vmem_limit_bytes=58 * 2**20
        ),
    )(queries, keys, values, frame_mask, frame_slot, out_weight, residual, gate.reshape(1, COLS))


def solution(mesh):
    fine = Mesh(mesh.devices.reshape(2, NY, NZ, 2, 2), AXES)
    wide, head = ("xl", "y", "z"), ("xh", "core")
    return jax.shard_map(
        _on_device,
        mesh=fine,
        in_specs=(
            P(wide, head),
            P(wide, head),
            P(wide, head),
            P(wide, None),
            P(),
            P(head, wide),
            P(wide, head),
            P(head),
        ),
        out_specs=P(wide, head),
        check_vma=False,
    )
```

```python
import functools
import math

import jax
import jax.numpy as jnp
from jax import lax
from jax.experimental import pallas as pl
from jax.experimental.pallas import tpu as pltpu
from jax.sharding import Mesh, PartitionSpec as P

HSIZE = 128
TOKF = 64
MESH = pl.DeviceIdType.MESH
AXES = ("xl", "y", "z", "xh", "core")
NY, NZ = 4, 8
NG = 8
CHUNK = NG * TOKF
HIDDEN = -1e30
FLOOR = -1e29
LOG2E_SCALE = 1.0 / (math.log(2.0) * math.sqrt(HSIZE))
ROWS = 384
FEATS = 4096
COLS = 1024
OWN = 512
STREAM = 4
ORDER = (0, 2, 1, 3)
PLACE = {(dy, o): 2 * i + o for i, dy in enumerate(ORDER) for o in range(2)}
PLANE = tuple((dy, o) for dy in ORDER for o in range(2) if (dy, o) != (0, 0))


def _kernel(
    q_ref, k_ref, v_ref, mask_ref, slot_ref, w_ref, res_ref, gate_ref, out_ref,
    k2, vbuf, vt, qbuf, bnd, bbuf, qt, m_sc, l_sc, acc, satt, att, wt, res, res2, upd, psum,
    loc, ka_s, ka_r, va_s, va_r, q_s, q_r, b_s, b_r, kv_s, kv_r,
    wx_s, wx_r, wr_s, wr_r, wn_s, wn_r, wy_s, wy_r, rl_s,
    t1_s, t1_r, t2_s, t2_r, t3_s, t3_r, sb_s, sb_r, rs_s, rs_r, up_s, up_r,
):
    xl, y, z = lax.axis_index("xl"), lax.axis_index("y"), lax.axis_index("z")
    xh, core = lax.axis_index("xh"), lax.axis_index("core")
    g = xl * NY + y
    head = xh * 2 + core
    ylo = lax.rem(y, 2)
    home = jnp.logical_and(core == y // 2, xl == ylo)

    def ypos(d):
        return lax.rem(y + d + NY, NY)

    def zpos(d):
        return lax.rem(z + d + NZ, NZ)

    def dev(other_xl=0, dy=0, dz=0, other_xh=0, other_core=0):
        return (
            1 - xl if other_xl else xl,
            ypos(dy),
            zpos(dz),
            1 - xh if other_xh else xh,
            1 - core if other_core else core,
        )

    def remote(src, dst, s, r, to):
        return pltpu.make_async_remote_copy(
            src_ref=src, dst_ref=dst, send_sem=s, recv_sem=r, device_id=to, device_id_type=MESH
        )

    sibling = dev(other_core=1)

    bar = pltpu.get_barrier_semaphore()
    peers = [dev(other_xl=o, dy=dy) for dy, o in PLANE]
    peers += [dev(dz=1), dev(dz=-1), sibling]
    peers += [dev(other_xl=o, other_xh=1) for o in (0, 1)]
    peers += [dev(other_xl=o, other_xh=h, other_core=1) for o, h in ((0, 1), (1, 0), (1, 1))]
    for to in peers:
        pl.semaphore_signal(bar, 1, device_id=to, device_id_type=MESH)

    def own_copy(src, dst, i):
        return pltpu.make_async_copy(src, dst, loc.at[i])

    bnd[...] = jnp.broadcast_to(
        jnp.sum(mask_ref[...], axis=0, keepdims=True).astype(jnp.float32), (8, ROWS)
    )
    bbuf[PLACE[(0, 0)]] = bnd[...]
    pl.semaphore_wait(bar, len(peers))

    def feat_cols(h):
        return pl.ds(pl.multiple_of(h * COLS, COLS), COLS)

    wx_copy = remote(w_ref, wt.at[z, :, feat_cols(head)], wx_s, wx_r.at[head], (ylo, y, z, xl, y // 2))
    wx_own = pltpu.make_async_copy(w_ref, wt.at[z, :, feat_cols(head)], wx_r.at[head])
    wx_is_self = jnp.logical_and(home, xl == xh)

    def tok_rows(i):
        return pl.ds(pl.multiple_of(i * TOKF, TOKF), TOKF)

    def head_cols(i):
        return pl.ds(pl.multiple_of(i * HSIZE, HSIZE), HSIZE)

    def group(dy, o):
        return (1 - xl if o else xl) * NY + ypos(dy)

    def k_copy(i, dy, o, src_g):
        return remote(
            k_ref.at[:, head_cols(group(dy, o))], k2.at[z, tok_rows(src_g), 0:HSIZE],
            ka_s.at[i], ka_r.at[i], dev(other_xl=o, dy=dy),
        )

    def v_copy(i, dy, o, src_g):
        return remote(
            v_ref.at[:, head_cols(group(dy, o))], vbuf.at[z, tok_rows(src_g), :],
            va_s.at[i], va_r.at[i], dev(other_xl=o, dy=dy),
        )

    def q_copy(i, dy, o):
        return remote(
            q_ref.at[:, head_cols(group(dy, o))], qbuf.at[PLACE[(-dy % NY, o)]],
            q_s.at[i], q_r.at[i], dev(other_xl=o, dy=dy),
        )

    def b_copy(i, dy, o):
        return remote(bnd, bbuf.at[PLACE[(-dy % NY, o)]], b_s.at[i], b_r.at[i], dev(other_xl=o, dy=dy))

    def window(i):
        return pl.ds(pl.multiple_of(i * OWN, OWN), OWN)

    k_own = own_copy(k_ref.at[:, head_cols(g)], k2.at[z, tok_rows(g), 0:HSIZE], 0)
    v_own = own_copy(v_ref.at[:, head_cols(g)], vbuf.at[z, tok_rows(g), :], 1)
    q_own = own_copy(q_ref.at[:, head_cols(g)], qbuf.at[PLACE[(0, 0)]], 2)
    res_in = own_copy(res_ref.at[:, window(xl)], res, 3)
    partner = dev(other_xl=1)
    res_out = remote(res_ref.at[:, window(1 - xl)], res2, rs_s, rs_r, partner)
    for i, (dy, o) in enumerate(PLANE):
        k_copy(i, dy, o, g).start()
    for i, (dy, o) in enumerate(PLANE):
        v_copy(i, dy, o, g).start()
    k_own.start()
    v_own.start()

    @pl.when(wx_is_self)
    def _():
        wx_own.start()

    @pl.when(jnp.logical_not(wx_is_self))
    def _():
        wx_copy.start()

    for i, (dy, o) in enumerate(PLANE):
        q_copy(i, dy, o).start()
        b_copy(i, dy, o).start()
    q_own.start()
    res_in.start()
    res_out.start()

    lane = lax.broadcasted_iota(jnp.int32, (TOKF, HSIZE), 1)

    def fill(i, _):
        zi, bi = i // NG, lax.rem(i, NG)
        k2[zi, tok_rows(bi), HSIZE : 2 * HSIZE] = jnp.where(lane == slot_ref[bi * NZ + zi], 1.0, 0.0).astype(
            jnp.bfloat16
        )
        return 0

    lax.fori_loop(0, NZ * NG, fill, 0)
    m_sc[...] = jnp.full(m_sc.shape, FLOOR, jnp.float32)
    l_sc[...] = jnp.zeros(l_sc.shape, jnp.float32)
    acc[...] = jnp.zeros(acc.shape, jnp.float32)
    qt[HSIZE : 2 * HSIZE, :] = jnp.zeros((HSIZE, NG * ROWS), jnp.bfloat16)

    def ring_dirs(r, which):
        if r < 4:
            return (1, -1)
        return (1,) if which == 0 else (-1,)

    class Ring:
        def __init__(self, piece, s, r):
            self.piece, self.s, self.r = piece, s, r

        def copy(self, d, r, which, steps):
            ref = self.piece(lax.rem(z - d * steps + 2 * NZ, NZ), which)
            i = 0 if d == 1 else 1
            return remote(ref, ref, self.s.at[i, r, which], self.r.at[i, r, which], dev(dz=d))

        def send(self, d, r, which):
            return self.copy(d, r, which, r - 1)

        def begin(self, which):
            for d in ring_dirs(1, which):
                self.send(d, 1, which).start()

        def step(self, r, pieces=(0, 1), also=None):
            for which in pieces:
                for d in ring_dirs(r, which):
                    self.copy(d, r, which, r).wait_recv()
                    if r < 4 and d in ring_dirs(r + 1, which):
                        self.send(d, r + 1, which).start()
                    if also is not None:
                        also(d, which)

        def end(self):
            for r in range(1, 5):
                for which in range(2):
                    for d in ring_dirs(r, which):
                        self.send(d, r, which).wait_send()

    def half(which):
        return slice(32 * which, 32 * which + 32)

    kv_ring = Ring(lambda slot, w: vbuf.at[slot] if w else k2.at[slot, :, 0:HSIZE], kv_s, kv_r)
    def w_rows(parity, which):
        return pl.ds(pl.multiple_of(32 * parity + 16 * which, 16), 16)

    w_ring = Ring(lambda slot, w: wt.at[slot, w_rows(ylo, w)], wr_s, wr_r)

    def wn_copy(d, r, which, parity):
        ref = wt.at[lax.rem(z - d * r + 2 * NZ, NZ), w_rows(parity, which)]
        i = 0 if d == 1 else 1
        return remote(ref, ref, wn_s.at[i, r, which], wn_r.at[i, r, which], dev(dy=d * (1 - 2 * ylo)))

    def w_step(r, pieces=(0, 1)):
        w_ring.step(r, pieces, lambda d, which: wn_copy(d, r, which, ylo).start())

    def w_each(act):
        for r in range(1, 5):
            for which in range(2):
                for d in ring_dirs(r, which):
                    act(d, r, which)

    def wy_copy(which, d, s):
        ref = wt.at[z, half(which)]
        return remote(ref, ref, s, wy_r.at[which], dev(dy=d))

    def wy_send(which, i):
        return wy_copy(which, (1, -1)[i], wy_s.at[which, i])

    place = lax.rem(y - 2 * core - xl + 2 * NY, NY)

    def relay_copy(which):
        return wy_copy(which, (1, -1)[which], rl_s)

    def relay():
        for which in range(2):

            @pl.when(place == (1, 3)[which])
            def _():
                wy_copy(which, 1, rl_s).wait_recv()
                relay_copy(which).start()

    def relayed():
        for which in range(2):

            @pl.when(jnp.logical_or(place == 2, place == (3, 1)[which]))
            def _():
                wy_copy(which, 1, rl_s).wait_recv()

    for i, (dy, o) in enumerate(PLANE):
        k_copy(i, dy, o, group(-dy, o)).wait_recv()
    k_own.wait()
    kv_ring.begin(0)
    for i, (dy, o) in enumerate(PLANE):
        v_copy(i, dy, o, group(-dy, o)).wait_recv()
    v_own.wait()
    kv_ring.begin(1)

    @pl.when(home)
    def _():
        for h in range(4):
            ref = wt.at[z, :, feat_cols(h)]
            pltpu.make_async_copy(ref, ref, wx_r.at[h]).wait()
        for which in range(2):
            for i in range(2):
                wy_send(which, i).start()

    kv_ring.step(1)
    relay()

    def queries_in(p):
        cols = slice(p * ROWS, (p + 1) * ROWS)
        qt[0:HSIZE, cols] = qbuf[p].T
        frame = lax.broadcasted_iota(jnp.int32, (TOKF, ROWS), 0).astype(jnp.float32)
        qt[HSIZE : HSIZE + TOKF, cols] = jnp.where(frame < bbuf[p, 0:1, :], 0.0, HIDDEN).astype(
            jnp.bfloat16
        )

    def queries(first, last):
        for i, (dy, o) in enumerate(PLANE):
            p = PLACE[(-dy % NY, o)]
            if first <= p < last:
                q_copy(i, dy, o).wait_recv()
                b_copy(i, dy, o).wait_recv()
                queries_in(p)
        if first <= PLACE[(0, 0)] < last:
            q_own.wait()
            queries_in(PLACE[(0, 0)])

    def vt_cols(slot):
        return pl.ds(pl.multiple_of(slot * CHUNK, CHUNK), CHUNK)

    def attend(n):
        slot = zpos((0, -1, 1, -2, 2, -3, 3, 4)[n])
        vt[:, vt_cols(slot)] = vbuf[slot].T
        s = jnp.dot(k2[slot], qt[:, 0 : STREAM * ROWS], preferred_element_type=jnp.float32)
        m_old = m_sc[0:1, :]
        m_new = jnp.maximum(m_old, jnp.max(s, axis=0, keepdims=True))
        p = jnp.exp2((s - m_new) * LOG2E_SCALE)
        shrink = jnp.exp2((m_old - m_new) * LOG2E_SCALE)
        m_sc[0:1, :] = m_new
        l_sc[0:1, :] = l_sc[0:1, :] * shrink + jnp.sum(p, axis=0, keepdims=True)
        acc[...] = acc[...] * shrink + jnp.dot(
            vt[:, vt_cols(slot)], p.astype(jnp.bfloat16), preferred_element_type=jnp.float32
        )

    def head_slot(other_xl, other_xh, dy, other_core=0, part=None):
        h = (1 - xh if other_xh else xh) * 2 + (1 - core if other_core else core)
        p = h * NG + (1 - xl if other_xl else xl) * NY + ypos(-dy)
        if part is None:
            return att.at[pl.ds(pl.multiple_of(p * HSIZE, HSIZE), HSIZE), :]
        return att.at[pl.ds(pl.multiple_of(p * HSIZE + part * 64, 64), 64), :]

    def t1_copy(dy):
        return remote(satt.at[dy], head_slot(0, 0, 0), t1_s.at[dy], t1_r.at[dy], dev(dy=dy))

    def t1_got(dy):
        return remote(satt.at[dy], head_slot(0, 0, dy), t1_s.at[dy], t1_r.at[dy], sibling)

    def t2_copy(dy, h):
        src = head_slot(0, 0, dy) if dy else satt.at[0]
        return remote(src, head_slot(0, 0, dy), t2_s.at[dy, h], t2_r.at[dy, h], dev(other_xl=1, other_xh=h))

    def t2_got(dy, h):
        ref = head_slot(1, h, dy)
        return remote(ref, ref, t2_s.at[dy, h], t2_r.at[dy, h], sibling)

    def t3_copy(dy, h):
        ref = head_slot(1, h, dy, part=h)
        return remote(ref, ref, t3_s.at[dy, h], t3_r.at[dy, h], dev(other_xl=1, other_xh=1 - h))

    def t3_got(dy, h):
        ref = head_slot(0, 1, dy, part=h)
        return remote(ref, ref, t3_s.at[dy, h], t3_r.at[dy, h], sibling)

    def sb_copy(dy, o, h):
        ref = head_slot(o, h, dy)
        return remote(ref, ref, sb_s.at[dy, o, h], sb_r.at[dy, o, h], sibling)

    def sb_got(dy, o, h):
        ref = head_slot(o, h, dy, 1)
        return remote(ref, ref, sb_s.at[dy, o, h], sb_r.at[dy, o, h], sibling)

    att_own = own_copy(satt.at[0], head_slot(0, 0, 0), 4)

    def give(dy):
        if dy:
            t1_copy(dy).start()
        else:
            for h in range(2):
                t2_copy(0, h).start()
            att_own.start()

    def pass_on(dy):
        if dy:
            t1_got(dy).wait_recv()
            for h in range(2):
                t2_copy(dy, h).start()
        else:
            att_own.wait()
        sb_copy(dy, 0, 0).start()

    def take(dy):
        for h in range(2):
            t2_got(dy, h).wait_recv()
            t3_copy(dy, h).start()
            sb_copy(dy, 1, h).start()

    def take_far(dy):
        for h in range(2):
            t3_got(dy, h).wait_recv()
        sb_copy(dy, 0, 1).start()

    def normed(p, mixed, total):
        dy, o = ORDER[p // 2], p % 2
        empty = (bbuf[p, 0:1, :] == 0.0).astype(jnp.float32)
        cols = pl.ds(pl.multiple_of((1 - xl if o else xl) * ROWS, ROWS), ROWS)
        satt[dy, :, cols] = (mixed / (total + empty)).astype(jnp.bfloat16)

    def attend_block(p):
        queries(p, p + 1)
        s = jnp.dot(
            k2[...].reshape(NZ * CHUNK, 2 * HSIZE),
            qt[:, p * ROWS : (p + 1) * ROWS],
            preferred_element_type=jnp.float32,
        )
        m_all = jnp.maximum(jnp.max(s, axis=0, keepdims=True), FLOOR)
        w = jnp.exp2((s - m_all) * LOG2E_SCALE)
        total = jnp.sum(w, axis=0, keepdims=True)
        mixed = jnp.dot(vt[...], w.astype(jnp.bfloat16), preferred_element_type=jnp.float32)
        normed(p, mixed, total)

    kv_ring.step(2)
    relayed()
    queries(0, STREAM)
    attend(0)
    kv_ring.step(3)
    w_ring.begin(0)
    w_ring.begin(1)
    attend(1)
    attend(2)
    attend(3)
    attend(4)
    kv_ring.step(4)
    attend(5)
    attend(6)
    attend(7)
    for p in range(STREAM):
        cols = slice(p * ROWS, (p + 1) * ROWS)
        normed(p, acc[:, cols], l_sc[0:1, cols])
        if p % 2:
            give(ORDER[p // 2])
    attend_block(4)
    w_step(1)
    pass_on(ORDER[1])
    pass_on(ORDER[0])
    attend_block(5)
    give(ORDER[2])
    take(ORDER[0])
    attend_block(6)
    w_step(2)
    pass_on(ORDER[2])
    take(ORDER[1])
    attend_block(7)
    give(ORDER[3])
    take_far(ORDER[0])
    w_step(3)
    take(ORDER[2])
    pass_on(ORDER[3])
    take_far(ORDER[1])
    w_step(4)
    take_far(ORDER[2])
    take(ORDER[3])
    take_far(ORDER[3])
    w_each(lambda d, r, which: wn_copy(d, r, which, 1 - ylo).wait_recv())

    def side_rows(side):
        return pl.ds(pl.multiple_of(side * ROWS, ROWS), ROWS)

    def project(i, side, c):
        total = None
        for h in (c, 2 + c):
            w = wt[4 * i : 4 * i + 4, :, feat_cols(h)].reshape(256, COLS)
            part = jnp.dot(w, att[feat_cols(h), side_rows(side)], preferred_element_type=jnp.float32)
            total = part if total is None else total + part
        return total

    def finish(i, side, before):
        summed = psum[2 * i + (0 if before is res2 else 1)] + project(i, side, 1 - core)
        scale = jnp.tanh(gate_ref[:, pl.ds(pl.multiple_of(xl * OWN + i * 256, 256), 256)])
        old = before[:, 256 * i : 256 * i + 256].astype(jnp.float32)
        return (old + scale * summed.T).astype(jnp.bfloat16)

    for i in range(2):
        psum[2 * i] = project(i, 1 - xl, core)
        psum[2 * i + 1] = project(i, xl, core)
    for dy in ORDER:
        for o in range(2):
            for h in range(2):
                sb_got(dy, o, h).wait_recv()
    res_in.wait()
    res_out.wait_recv()

    def up_copy(i):
        cols = pl.ds(pl.multiple_of(xl * OWN + i * 256, 256), 256)
        return remote(upd.at[i], out_ref.at[:, cols], up_s.at[i], up_r.at[i], partner)

    def up_got(i):
        cols = pl.ds(pl.multiple_of((1 - xl) * OWN + i * 256, 256), 256)
        return remote(upd.at[i], out_ref.at[:, cols], up_s.at[i], up_r.at[i], partner)

    for i in range(2):
        upd[i] = finish(i, 1 - xl, res2)
        up_copy(i).start()
    for i in range(2):
        out_ref[:, pl.ds(pl.multiple_of(xl * OWN + i * 256, 256), 256)] = finish(i, xl, res)
    for i in range(2):
        up_got(i).wait_recv()

    @pl.when(jnp.logical_not(wx_is_self))
    def _():
        wx_copy.wait_send()

    for i, (dy, o) in enumerate(PLANE):
        k_copy(i, dy, o, g).wait_send()
        v_copy(i, dy, o, g).wait_send()
        q_copy(i, dy, o).wait_send()
        b_copy(i, dy, o).wait_send()
    res_out.wait_send()
    kv_ring.end()

    w_ring.end()
    w_each(lambda d, r, which: wn_copy(d, r, which, ylo).wait_send())

    @pl.when(home)
    def _():
        for which in range(2):
            for i in range(2):
                wy_send(which, i).wait_send()

    for which in range(2):

        @pl.when(place == (1, 3)[which])
        def _():
            relay_copy(which).wait_send()

    for dy in ORDER:
        if dy:
            t1_copy(dy).wait_send()
        for h in range(2):
            t2_copy(dy, h).wait_send()
            t3_copy(dy, h).wait_send()
            for o in range(2):
                sb_copy(dy, o, h).wait_send()
    for i in range(2):
        up_copy(i).wait_send()


def _on_device(queries, keys, values, frame_mask, frame_slot, out_weight, residual, gate):
    dma = pltpu.SemaphoreType.DMA
    vmem = pl.BlockSpec(memory_space=pltpu.VMEM)
    hbm = pl.BlockSpec(memory_space=pl.ANY)
    smem = pl.BlockSpec(memory_space=pltpu.SMEM)
    bf16, f32 = jnp.bfloat16, jnp.float32
    return pl.pallas_call(
        _kernel,
        out_shape=jax.ShapeDtypeStruct((ROWS, COLS), bf16),
        in_specs=[hbm, hbm, hbm, vmem, smem, vmem, hbm, vmem],
        out_specs=vmem,
        scratch_shapes=[
            pltpu.VMEM((NZ, CHUNK, 2 * HSIZE), bf16),
            pltpu.VMEM((NZ, CHUNK, HSIZE), bf16),
            pltpu.VMEM((HSIZE, NZ * CHUNK), bf16),
            pltpu.VMEM((NG, ROWS, HSIZE), bf16),
            pltpu.VMEM((8, ROWS), f32),
            pltpu.VMEM((NG, 8, ROWS), f32),
            pltpu.VMEM((2 * HSIZE, NG * ROWS), bf16),
            pltpu.VMEM((8, STREAM * ROWS), f32),
            pltpu.VMEM((8, STREAM * ROWS), f32),
            pltpu.VMEM((HSIZE, STREAM * ROWS), f32),
            pltpu.VMEM((NY, HSIZE, 2 * ROWS), bf16),
            pltpu.VMEM((FEATS, 2 * ROWS), bf16),
            pltpu.VMEM((NZ, TOKF, FEATS), bf16),
            pltpu.VMEM((ROWS, OWN), bf16),
            pltpu.VMEM((ROWS, OWN), bf16),
            pltpu.VMEM((2, ROWS, 256), bf16),
            pltpu.VMEM((4, 256, ROWS), f32),
            dma((5,)),
            dma((7,)), dma((7,)), dma((7,)), dma((7,)),
            dma((7,)), dma((7,)), dma((7,)), dma((7,)),
            dma((2, 5, 2)), dma((2, 5, 2)),
            dma, dma((4,)),
            dma((2, 5, 2)), dma((2, 5, 2)),
            dma((2, 5, 2)), dma((2, 5, 2)),
            dma((2, 2)), dma((2,)), dma,
            dma((4,)), dma((4,)),
            dma((4, 2)), dma((4, 2)),
            dma((4, 2)), dma((4, 2)),
            dma((4, 2, 2)), dma((4, 2, 2)),
            dma, dma,
            dma((2,)), dma((2,)),
        ],
        compiler_params=pltpu.CompilerParams(
            collective_id=0, has_side_effects=True, vmem_limit_bytes=58 * 2**20
        ),
    )(queries, keys, values, frame_mask.T, frame_slot, out_weight.T, residual, gate.reshape(1, COLS))


def solution(mesh):
    fine = Mesh(mesh.devices.reshape(2, NY, NZ, 2, 2), AXES)
    wide, head = ("xl", "y", "z"), ("xh", "core")
    return jax.shard_map(
        _on_device,
        mesh=fine,
        in_specs=(
            P(wide, head),
            P(wide, head),
            P(wide, head),
            P(wide, None),
            P(),
            P(head, wide),
            P(wide, head),
            P(head),
        ),
        out_specs=P(wide, head),
        check_vma=False,
    )
```

```python
import functools
import math

import jax
import jax.numpy as jnp
from jax import lax
from jax.experimental import pallas as pl
from jax.experimental.pallas import tpu as pltpu
from jax.sharding import Mesh, PartitionSpec as P

HSIZE = 128
TOKF = 64
MESH = pl.DeviceIdType.MESH
AXES = ("xl", "y", "z", "xh", "core")
NY, NZ = 4, 8
NG = 8
CHUNK = NG * TOKF
HIDDEN = -1e30
FLOOR = -1e29
LOG2E_SCALE = 1.0 / (math.log(2.0) * math.sqrt(HSIZE))
ROWS = 384
FEATS = 4096
COLS = 1024
OWN = 512
STREAM = 4
ORDER = (0, 2, 1, 3)
PLACE = {(dy, o): 2 * i + o for i, dy in enumerate(ORDER) for o in range(2)}
PLANE = tuple((dy, o) for dy in ORDER for o in range(2) if (dy, o) != (0, 0))


def _kernel(
    q_ref, k_ref, v_ref, mask_ref, slot_ref, w_ref, res_ref, gate_ref, out_ref,
    k2, vbuf, vt, qbuf, bnd, bbuf, qt, m_sc, l_sc, acc, satt, att, wt, res, res2, upd, psum,
    loc, ka_s, ka_r, va_s, va_r, q_s, q_r, b_s, b_r, kv_s, kv_r,
    wx_s, wx_r, wr_s, wr_r, wn_s, wn_r, wy_s, wy_r, rl_s,
    t1_s, t1_r, t2_s, t2_r, t3_s, t3_r, sb_s, sb_r, rs_s, rs_r, up_s, up_r,
):
    xl, y, z = lax.axis_index("xl"), lax.axis_index("y"), lax.axis_index("z")
    xh, core = lax.axis_index("xh"), lax.axis_index("core")
    g = xl * NY + y
    head = xh * 2 + core
    ylo = lax.rem(y, 2)
    home = jnp.logical_and(core == y // 2, xl == ylo)

    def ypos(d):
        return lax.rem(y + d + NY, NY)

    def zpos(d):
        return lax.rem(z + d + NZ, NZ)

    def dev(other_xl=0, dy=0, dz=0, other_xh=0, other_core=0):
        return (
            1 - xl if other_xl else xl,
            ypos(dy),
            zpos(dz),
            1 - xh if other_xh else xh,
            1 - core if other_core else core,
        )

    def remote(src, dst, s, r, to):
        return pltpu.make_async_remote_copy(
            src_ref=src, dst_ref=dst, send_sem=s, recv_sem=r, device_id=to, device_id_type=MESH
        )

    sibling = dev(other_core=1)

    bar = pltpu.get_barrier_semaphore()
    peers = [dev(other_xl=o, dy=dy) for dy, o in PLANE]
    peers += [dev(dz=1), dev(dz=-1), sibling]
    peers += [dev(other_xl=o, other_xh=1) for o in (0, 1)]
    peers += [dev(other_xl=o, other_xh=h, other_core=1) for o, h in ((0, 1), (1, 0), (1, 1))]
    for to in peers:
        pl.semaphore_signal(bar, 1, device_id=to, device_id_type=MESH)

    def own_copy(src, dst, i):
        return pltpu.make_async_copy(src, dst, loc.at[i])

    bnd[...] = jnp.broadcast_to(
        jnp.sum(mask_ref[...], axis=0, keepdims=True).astype(jnp.float32), (8, ROWS)
    )
    bbuf[PLACE[(0, 0)]] = bnd[...]
    pl.semaphore_wait(bar, len(peers))

    def feat_cols(h):
        return pl.ds(pl.multiple_of(h * COLS, COLS), COLS)

    wx_copy = remote(w_ref, wt.at[z, :, feat_cols(head)], wx_s, wx_r.at[head], (ylo, y, z, xl, y // 2))
    wx_own = pltpu.make_async_copy(w_ref, wt.at[z, :, feat_cols(head)], wx_r.at[head])
    wx_is_self = jnp.logical_and(home, xl == xh)

    def tok_rows(i):
        return pl.ds(pl.multiple_of(i * TOKF, TOKF), TOKF)

    def head_cols(i):
        return pl.ds(pl.multiple_of(i * HSIZE, HSIZE), HSIZE)

    def group(dy, o):
        return (1 - xl if o else xl) * NY + ypos(dy)

    def k_copy(i, dy, o, src_g):
        return remote(
            k_ref.at[:, head_cols(group(dy, o))], k2.at[z, tok_rows(src_g), 0:HSIZE],
            ka_s.at[i], ka_r.at[i], dev(other_xl=o, dy=dy),
        )

    def v_copy(i, dy, o, src_g):
        return remote(
            v_ref.at[:, head_cols(group(dy, o))], vbuf.at[z, tok_rows(src_g), :],
            va_s.at[i], va_r.at[i], dev(other_xl=o, dy=dy),
        )

    def q_copy(i, dy, o):
        return remote(
            q_ref.at[:, head_cols(group(dy, o))], qbuf.at[PLACE[(-dy % NY, o)]],
            q_s.at[i], q_r.at[i], dev(other_xl=o, dy=dy),
        )

    def b_copy(i, dy, o):
        return remote(bnd, bbuf.at[PLACE[(-dy % NY, o)]], b_s.at[i], b_r.at[i], dev(other_xl=o, dy=dy))

    def window(i):
        return pl.ds(pl.multiple_of(i * OWN, OWN), OWN)

    k_own = own_copy(k_ref.at[:, head_cols(g)], k2.at[z, tok_rows(g), 0:HSIZE], 0)
    v_own = own_copy(v_ref.at[:, head_cols(g)], vbuf.at[z, tok_rows(g), :], 1)
    q_own = own_copy(q_ref.at[:, head_cols(g)], qbuf.at[PLACE[(0, 0)]], 2)
    res_in = own_copy(res_ref.at[:, window(xl)], res, 3)
    partner = dev(other_xl=1)
    res_out = remote(res_ref.at[:, window(1 - xl)], res2, rs_s, rs_r, partner)
    for i, (dy, o) in enumerate(PLANE):
        k_copy(i, dy, o, g).start()
    for i, (dy, o) in enumerate(PLANE):
        v_copy(i, dy, o, g).start()
    k_own.start()
    v_own.start()

    @pl.when(wx_is_self)
    def _():
        wx_own.start()

    @pl.when(jnp.logical_not(wx_is_self))
    def _():
        wx_copy.start()

    for i, (dy, o) in enumerate(PLANE):
        q_copy(i, dy, o).start()
        b_copy(i, dy, o).start()
    q_own.start()
    res_in.start()

    lane = lax.broadcasted_iota(jnp.int32, (TOKF, HSIZE), 1)

    def fill(i, _):
        zi, bi = i // NG, lax.rem(i, NG)
        k2[zi, tok_rows(bi), HSIZE : 2 * HSIZE] = jnp.where(lane == slot_ref[bi * NZ + zi], 1.0, 0.0).astype(
            jnp.bfloat16
        )
        return 0

    lax.fori_loop(0, NZ * NG, fill, 0)
    m_sc[...] = jnp.full(m_sc.shape, FLOOR, jnp.float32)
    l_sc[...] = jnp.zeros(l_sc.shape, jnp.float32)
    acc[...] = jnp.zeros(acc.shape, jnp.float32)
    qt[HSIZE : 2 * HSIZE, :] = jnp.zeros((HSIZE, NG * ROWS), jnp.bfloat16)

    def ring_dirs(r, which):
        if r < 4:
            return (1, -1)
        return (1,) if which == 0 else (-1,)

    class Ring:
        def __init__(self, piece, s, r):
            self.piece, self.s, self.r = piece, s, r

        def copy(self, d, r, which, steps):
            ref = self.piece(lax.rem(z - d * steps + 2 * NZ, NZ), which)
            i = 0 if d == 1 else 1
            return remote(ref, ref, self.s.at[i, r, which], self.r.at[i, r, which], dev(dz=d))

        def send(self, d, r, which):
            return self.copy(d, r, which, r - 1)

        def begin(self, which):
            for d in ring_dirs(1, which):
                self.send(d, 1, which).start()

        def step(self, r, pieces=(0, 1), also=None):
            for which in pieces:
                for d in ring_dirs(r, which):
                    self.copy(d, r, which, r).wait_recv()
                    if r < 4 and d in ring_dirs(r + 1, which):
                        self.send(d, r + 1, which).start()
                    if also is not None:
                        also(d, which)

        def end(self):
            for r in range(1, 5):
                for which in range(2):
                    for d in ring_dirs(r, which):
                        self.send(d, r, which).wait_send()

    def half(which):
        return slice(32 * which, 32 * which + 32)

    kv_ring = Ring(lambda slot, w: vbuf.at[slot] if w else k2.at[slot, :, 0:HSIZE], kv_s, kv_r)
    def w_rows(parity, which):
        return pl.ds(pl.multiple_of(32 * parity + 16 * which, 16), 16)

    w_ring = Ring(lambda slot, w: wt.at[slot, w_rows(ylo, w)], wr_s, wr_r)

    def wn_copy(d, r, which, parity):
        ref = wt.at[lax.rem(z - d * r + 2 * NZ, NZ), w_rows(parity, which)]
        i = 0 if d == 1 else 1
        return remote(ref, ref, wn_s.at[i, r, which], wn_r.at[i, r, which], dev(dy=d * (1 - 2 * ylo)))

    def w_step(r, pieces=(0, 1)):
        w_ring.step(r, pieces, lambda d, which: wn_copy(d, r, which, ylo).start())

    def w_each(act):
        for r in range(1, 5):
            for which in range(2):
                for d in ring_dirs(r, which):
                    act(d, r, which)

    def wy_copy(which, d, s):
        ref = wt.at[z, half(which)]
        return remote(ref, ref, s, wy_r.at[which], dev(dy=d))

    def wy_send(which, i):
        return wy_copy(which, (1, -1)[i], wy_s.at[which, i])

    place = lax.rem(y - 2 * core - xl + 2 * NY, NY)

    def relay_copy(which):
        return wy_copy(which, (1, -1)[which], rl_s)

    def relay():
        for which in range(2):

            @pl.when(place == (1, 3)[which])
            def _():
                wy_copy(which, 1, rl_s).wait_recv()
                relay_copy(which).start()

    def relayed():
        for which in range(2):

            @pl.when(jnp.logical_or(place == 2, place == (3, 1)[which]))
            def _():
                wy_copy(which, 1, rl_s).wait_recv()

    for i, (dy, o) in enumerate(PLANE):
        k_copy(i, dy, o, group(-dy, o)).wait_recv()
    k_own.wait()
    kv_ring.begin(0)
    for i, (dy, o) in enumerate(PLANE):
        v_copy(i, dy, o, group(-dy, o)).wait_recv()
    v_own.wait()
    kv_ring.begin(1)

    @pl.when(home)
    def _():
        for h in range(4):
            ref = wt.at[z, :, feat_cols(h)]
            pltpu.make_async_copy(ref, ref, wx_r.at[h]).wait()
        for which in range(2):
            for i in range(2):
                wy_send(which, i).start()

    kv_ring.step(1)
    relay()

    def queries_in(p):
        cols = slice(p * ROWS, (p + 1) * ROWS)
        qt[0:HSIZE, cols] = qbuf[p].T
        frame = lax.broadcasted_iota(jnp.int32, (TOKF, ROWS), 0).astype(jnp.float32)
        qt[HSIZE : HSIZE + TOKF, cols] = jnp.where(frame < bbuf[p, 0:1, :], 0.0, HIDDEN).astype(
            jnp.bfloat16
        )

    def queries(first, last):
        for i, (dy, o) in enumerate(PLANE):
            p = PLACE[(-dy % NY, o)]
            if first <= p < last:
                q_copy(i, dy, o).wait_recv()
                b_copy(i, dy, o).wait_recv()
                queries_in(p)
        if first <= PLACE[(0, 0)] < last:
            q_own.wait()
            queries_in(PLACE[(0, 0)])

    def vt_cols(slot):
        return pl.ds(pl.multiple_of(slot * CHUNK, CHUNK), CHUNK)

    def attend(n):
        slot = zpos((0, -1, 1, -2, 2, -3, 3, 4)[n])
        vt[:, vt_cols(slot)] = vbuf[slot].T
        s = jnp.dot(k2[slot], qt[:, 0 : STREAM * ROWS], preferred_element_type=jnp.float32)
        m_old = m_sc[0:1, :]
        m_new = jnp.maximum(m_old, jnp.max(s, axis=0, keepdims=True))
        p = jnp.exp2((s - m_new) * LOG2E_SCALE)
        shrink = jnp.exp2((m_old - m_new) * LOG2E_SCALE)
        m_sc[0:1, :] = m_new
        l_sc[0:1, :] = l_sc[0:1, :] * shrink + jnp.sum(p, axis=0, keepdims=True)
        acc[...] = acc[...] * shrink + jnp.dot(
            vt[:, vt_cols(slot)], p.astype(jnp.bfloat16), preferred_element_type=jnp.float32
        )

    def head_slot(other_xl, other_xh, dy, other_core=0, part=None):
        h = (1 - xh if other_xh else xh) * 2 + (1 - core if other_core else core)
        p = h * NG + (1 - xl if other_xl else xl) * NY + ypos(-dy)
        if part is None:
            return att.at[pl.ds(pl.multiple_of(p * HSIZE, HSIZE), HSIZE), :]
        return att.at[pl.ds(pl.multiple_of(p * HSIZE + part * 64, 64), 64), :]

    def t1_copy(dy):
        return remote(satt.at[dy], head_slot(0, 0, 0), t1_s.at[dy], t1_r.at[dy], dev(dy=dy))

    def t1_got(dy):
        return remote(satt.at[dy], head_slot(0, 0, dy), t1_s.at[dy], t1_r.at[dy], sibling)

    def t2_copy(dy, h):
        src = head_slot(0, 0, dy) if dy else satt.at[0]
        return remote(src, head_slot(0, 0, dy), t2_s.at[dy, h], t2_r.at[dy, h], dev(other_xl=1, other_xh=h))

    def t2_got(dy, h):
        ref = head_slot(1, h, dy)
        return remote(ref, ref, t2_s.at[dy, h], t2_r.at[dy, h], sibling)

    def t3_copy(dy, h):
        ref = head_slot(1, h, dy, part=h)
        return remote(ref, ref, t3_s.at[dy, h], t3_r.at[dy, h], dev(other_xl=1, other_xh=1 - h))

    def t3_got(dy, h):
        ref = head_slot(0, 1, dy, part=h)
        return remote(ref, ref, t3_s.at[dy, h], t3_r.at[dy, h], sibling)

    def sb_copy(dy, o, h):
        ref = head_slot(o, h, dy)
        return remote(ref, ref, sb_s.at[dy, o, h], sb_r.at[dy, o, h], sibling)

    def sb_got(dy, o, h):
        ref = head_slot(o, h, dy, 1)
        return remote(ref, ref, sb_s.at[dy, o, h], sb_r.at[dy, o, h], sibling)

    att_own = own_copy(satt.at[0], head_slot(0, 0, 0), 4)

    def give(dy):
        if dy:
            t1_copy(dy).start()
        else:
            for h in range(2):
                t2_copy(0, h).start()
            att_own.start()

    def pass_on(dy):
        if dy:
            t1_got(dy).wait_recv()
            for h in range(2):
                t2_copy(dy, h).start()
        else:
            att_own.wait()
        sb_copy(dy, 0, 0).start()

    def take(dy):
        for h in range(2):
            t2_got(dy, h).wait_recv()
            t3_copy(dy, h).start()
            sb_copy(dy, 1, h).start()

    def take_far(dy):
        for h in range(2):
            t3_got(dy, h).wait_recv()
        sb_copy(dy, 0, 1).start()

    def normed(p, mixed, total):
        dy, o = ORDER[p // 2], p % 2
        empty = (bbuf[p, 0:1, :] == 0.0).astype(jnp.float32)
        cols = pl.ds(pl.multiple_of((1 - xl if o else xl) * ROWS, ROWS), ROWS)
        satt[dy, :, cols] = (mixed / (total + empty)).astype(jnp.bfloat16)

    def attend_block(p):
        queries(p, p + 1)
        s = jnp.dot(
            k2[...].reshape(NZ * CHUNK, 2 * HSIZE),
            qt[:, p * ROWS : (p + 1) * ROWS],
            preferred_element_type=jnp.float32,
        )
        m_all = jnp.maximum(jnp.max(s, axis=0, keepdims=True), FLOOR)
        w = jnp.exp2((s - m_all) * LOG2E_SCALE)
        total = jnp.sum(w, axis=0, keepdims=True)
        mixed = jnp.dot(vt[...], w.astype(jnp.bfloat16), preferred_element_type=jnp.float32)
        normed(p, mixed, total)

    kv_ring.step(2)
    relayed()
    queries(0, STREAM)
    res_out.start()
    attend(0)
    attend(1)
    attend(2)
    kv_ring.step(3)
    w_ring.begin(0)
    w_ring.begin(1)
    for n in range(3, 7):
        attend(n)
    kv_ring.step(4)
    attend(7)
    for p in range(STREAM):
        cols = slice(p * ROWS, (p + 1) * ROWS)
        normed(p, acc[:, cols], l_sc[0:1, cols])
        if p % 2:
            give(ORDER[p // 2])
    attend_block(4)
    w_step(1)
    pass_on(ORDER[1])
    pass_on(ORDER[0])
    attend_block(5)
    give(ORDER[2])
    take(ORDER[0])
    attend_block(6)
    w_step(2)
    pass_on(ORDER[2])
    attend_block(7)
    give(ORDER[3])
    take(ORDER[1])
    take_far(ORDER[0])
    w_step(3)
    take(ORDER[2])
    pass_on(ORDER[3])
    take_far(ORDER[1])
    w_step(4)
    take_far(ORDER[2])
    take(ORDER[3])
    take_far(ORDER[3])
    w_each(lambda d, r, which: wn_copy(d, r, which, 1 - ylo).wait_recv())

    def side_rows(side):
        return pl.ds(pl.multiple_of(side * ROWS, ROWS), ROWS)

    def project(i, side, c):
        total = None
        for h in (c, 2 + c):
            w = wt[4 * i : 4 * i + 4, :, feat_cols(h)].reshape(256, COLS)
            part = jnp.dot(w, att[feat_cols(h), side_rows(side)], preferred_element_type=jnp.float32)
            total = part if total is None else total + part
        return total

    def finish(i, side, before):
        summed = psum[2 * i + (0 if before is res2 else 1)] + project(i, side, 1 - core)
        scale = jnp.tanh(gate_ref[:, pl.ds(pl.multiple_of(xl * OWN + i * 256, 256), 256)])
        old = before[:, 256 * i : 256 * i + 256].astype(jnp.float32)
        return (old + scale * summed.T).astype(jnp.bfloat16)

    for i in range(2):
        psum[2 * i] = project(i, 1 - xl, core)
        psum[2 * i + 1] = project(i, xl, core)
    for dy in ORDER:
        for o in range(2):
            for h in range(2):
                sb_got(dy, o, h).wait_recv()
    res_in.wait()
    res_out.wait_recv()

    def up_copy(i):
        cols = pl.ds(pl.multiple_of(xl * OWN + i * 256, 256), 256)
        return remote(upd.at[i], out_ref.at[:, cols], up_s.at[i], up_r.at[i], partner)

    def up_got(i):
        cols = pl.ds(pl.multiple_of((1 - xl) * OWN + i * 256, 256), 256)
        return remote(upd.at[i], out_ref.at[:, cols], up_s.at[i], up_r.at[i], partner)

    for i in range(2):
        upd[i] = finish(i, 1 - xl, res2)
        up_copy(i).start()
    for i in range(2):
        out_ref[:, pl.ds(pl.multiple_of(xl * OWN + i * 256, 256), 256)] = finish(i, xl, res)
    for i in range(2):
        up_got(i).wait_recv()

    @pl.when(jnp.logical_not(wx_is_self))
    def _():
        wx_copy.wait_send()

    for i, (dy, o) in enumerate(PLANE):
        k_copy(i, dy, o, g).wait_send()
        v_copy(i, dy, o, g).wait_send()
        q_copy(i, dy, o).wait_send()
        b_copy(i, dy, o).wait_send()
    res_out.wait_send()
    kv_ring.end()

    w_ring.end()
    w_each(lambda d, r, which: wn_copy(d, r, which, ylo).wait_send())

    @pl.when(home)
    def _():
        for which in range(2):
            for i in range(2):
                wy_send(which, i).wait_send()

    for which in range(2):

        @pl.when(place == (1, 3)[which])
        def _():
            relay_copy(which).wait_send()

    for dy in ORDER:
        if dy:
            t1_copy(dy).wait_send()
        for h in range(2):
            t2_copy(dy, h).wait_send()
            t3_copy(dy, h).wait_send()
            for o in range(2):
                sb_copy(dy, o, h).wait_send()
    for i in range(2):
        up_copy(i).wait_send()


def _on_device(queries, keys, values, frame_mask, frame_slot, out_weight, residual, gate):
    dma = pltpu.SemaphoreType.DMA
    vmem = pl.BlockSpec(memory_space=pltpu.VMEM)
    hbm = pl.BlockSpec(memory_space=pl.ANY)
    smem = pl.BlockSpec(memory_space=pltpu.SMEM)
    bf16, f32 = jnp.bfloat16, jnp.float32
    return pl.pallas_call(
        _kernel,
        out_shape=jax.ShapeDtypeStruct((ROWS, COLS), bf16),
        in_specs=[hbm, hbm, hbm, vmem, smem, vmem, hbm, vmem],
        out_specs=vmem,
        scratch_shapes=[
            pltpu.VMEM((NZ, CHUNK, 2 * HSIZE), bf16),
            pltpu.VMEM((NZ, CHUNK, HSIZE), bf16),
            pltpu.VMEM((HSIZE, NZ * CHUNK), bf16),
            pltpu.VMEM((NG, ROWS, HSIZE), bf16),
            pltpu.VMEM((8, ROWS), f32),
            pltpu.VMEM((NG, 8, ROWS), f32),
            pltpu.VMEM((2 * HSIZE, NG * ROWS), bf16),
            pltpu.VMEM((8, STREAM * ROWS), f32),
            pltpu.VMEM((8, STREAM * ROWS), f32),
            pltpu.VMEM((HSIZE, STREAM * ROWS), f32),
            pltpu.VMEM((NY, HSIZE, 2 * ROWS), bf16),
            pltpu.VMEM((FEATS, 2 * ROWS), bf16),
            pltpu.VMEM((NZ, TOKF, FEATS), bf16),
            pltpu.VMEM((ROWS, OWN), bf16),
            pltpu.VMEM((ROWS, OWN), bf16),
            pltpu.VMEM((2, ROWS, 256), bf16),
            pltpu.VMEM((4, 256, ROWS), f32),
            dma((5,)),
            dma((7,)), dma((7,)), dma((7,)), dma((7,)),
            dma((7,)), dma((7,)), dma((7,)), dma((7,)),
            dma((2, 5, 2)), dma((2, 5, 2)),
            dma, dma((4,)),
            dma((2, 5, 2)), dma((2, 5, 2)),
            dma((2, 5, 2)), dma((2, 5, 2)),
            dma((2, 2)), dma((2,)), dma,
            dma((4,)), dma((4,)),
            dma((4, 2)), dma((4, 2)),
            dma((4, 2)), dma((4, 2)),
            dma((4, 2, 2)), dma((4, 2, 2)),
            dma, dma,
            dma((2,)), dma((2,)),
        ],
        compiler_params=pltpu.CompilerParams(
            collective_id=0, has_side_effects=True, vmem_limit_bytes=58 * 2**20
        ),
    )(queries, keys, values, frame_mask.T, frame_slot, out_weight.T, residual, gate.reshape(1, COLS))


def solution(mesh):
    fine = Mesh(mesh.devices.reshape(2, NY, NZ, 2, 2), AXES)
    wide, head = ("xl", "y", "z"), ("xh", "core")
    return jax.shard_map(
        _on_device,
        mesh=fine,
        in_specs=(
            P(wide, head),
            P(wide, head),
            P(wide, head),
            P(wide, None),
            P(),
            P(head, wide),
            P(wide, head),
            P(head),
        ),
        out_specs=P(wide, head),
        check_vma=False,
    )
```
